32 devices in a mesh: blk: 16 (over z, y, core), group: 2 (over x).
Axes of the slice: x: 2, y: 2, z: 4, core: 2. Of those that a mesh axis runs over, the one named last changes fastest.
Arguments:
- features: bfloat16 [2, 4096, 2048], P('group', 'blk'), may hold values from -0.29882812 to 0.29882812
- head_weight: bfloat16 [2048, 512], replicated, may hold values from -0.125 to 0.125
- pairs: int32 [2, 4096], P('group', 'blk'), may hold values from 0 to 4095, as said below
Outputs:
- pair_logit: float32 [2, 4096], P('group', 'blk')
- row_lse: float32 [2, 4096], P('group', 'blk')
- proj_grad: float32 [2, 4096, 512], P('group', 'blk')
- head_grad: float32 [2048, 512], replicated
The draws below stay inside these ranges and needn't reach their ends.
Inputs may be any that keep to these rules, and one draw needn't show every extreme that they name: pairs pairs each view with another view of the same group, and pairs[g, pairs[g, i]] = i.
All inputs are finite; a program needn't handle non-finite values.
Results may differ from the reference program's by a relative error of at most 0.004.
Values may be sent and summed in bfloat16 or wider, within the bound.
No kernel may reach another device: no remote copies, remote signals or barrier semaphores. Data moves between devices by JAX's collectives and lax.ppermute only.
A program may use at most 64 MiB of HBM per device.

```python
import jax
import jax.numpy as jnp
from jax import lax

HID = 2048
PROJ = 512
GROUPS = 2
VIEWS = 4096


def pair_one(key):
    perm = jax.random.permutation(key, VIEWS)
    swapped = perm.reshape(-1, 2)[:, ::-1].reshape(-1)
    return jnp.zeros((VIEWS,), jnp.int32).at[perm].set(swapped.astype(jnp.int32))


def draw_pairs(key, part):
    key = jax.random.fold_in(key, 1)
    keys = jax.random.split(key, GROUPS)
    return jax.vmap(pair_one)(keys).astype(jnp.int32)


def levels(rng, extent, cuts, least, high):
    def one(dim, shards_of):
        steps = jax.random.uniform(jax.random.fold_in(jax.random.fold_in(rng, 6), dim), (shards_of,), jnp.float32, least / len(cuts), high / len(cuts))
        return jnp.repeat(jnp.exp(steps), extent[dim] // shards_of).reshape((-1,) + (1,) * (len(extent) - dim - 1))

    gain = one(*cuts[0])
    for cut in cuts[1:]:
        gain = gain * one(*cut)
    return gain


def gaussian(own_key, dims, spread, limit, cuts=(), kind=jnp.bfloat16):
    level = levels(own_key, dims, cuts, -0.22, 0.18) if cuts else 1.0
    result = jax.random.normal(own_key, dims, jnp.float32) * spread * level
    return jnp.minimum(jnp.maximum(result, -limit), limit).astype(kind)


def setup_inputs(seed: int = 0) -> dict:
    streams_of = jax.random.split(jax.random.key(seed), 4)
    features = gaussian(streams_of[0], (GROUPS, VIEWS, HID), 0.05, 0.29882812, ((0, 2), (1, 16)))
    head_weight = gaussian(streams_of[1], (HID, PROJ), HID ** -0.5, 0.125)
    pairs = draw_pairs(jax.random.fold_in(streams_of[3], 71), 0)
    return {"features": features, "head_weight": head_weight, "pairs": pairs}


logit_divisor = 0.1

def one_group(args, head_weight):
    feats, pairs = args
    z = jnp.dot(feats, head_weight, preferred_element_type=jnp.float32)
    inv = lax.rsqrt(lax.optimization_barrier(jnp.sum(z * z, axis=1)) + 1e-06)
    u = z * inv[:, None]
    sphere_embeddings = u.astype(jnp.bfloat16)
    cosine_affinity = jnp.dot(sphere_embeddings, sphere_embeddings.T, preferred_element_type=jnp.float32) / logit_divisor
    count = cosine_affinity.shape[0]
    idx = jnp.arange(count, dtype=jnp.int32)
    e = jnp.where(idx[:, None] == idx[None, :], jnp.zeros_like(cosine_affinity), jnp.exp(cosine_affinity))
    den = lax.optimization_barrier(jnp.sum(e, axis=1))
    lse = jnp.log(den)
    pairmask = pairs[:, None] == idx[None, :]
    pos = lax.optimization_barrier(jnp.sum(jnp.where(pairmask, cosine_affinity, jnp.zeros_like(cosine_affinity)), axis=1))
    linear_map_coefficients = e / den[:, None] + e / den[None, :] - 2.0 * pairmask.astype(cosine_affinity.dtype)
    rescaled_direction_slope = jnp.dot(linear_map_coefficients.astype(jnp.bfloat16), sphere_embeddings, preferred_element_type=jnp.float32) / logit_divisor
    dz = inv[:, None] * (rescaled_direction_slope - u * lax.optimization_barrier(jnp.sum(u * rescaled_direction_slope, axis=1, keepdims=True)))
    head_term = jnp.dot(feats.T, dz.astype(jnp.bfloat16), preferred_element_type=jnp.float32)
    return (pos, lse, dz, head_term)

def reference(features, head_weight, pairs):
    pos, lse, dz, terms = lax.map(lambda a: one_group(a, head_weight), (features, pairs))
    return (pos, lse, dz, lax.optimization_barrier(jnp.sum(terms, axis=0)))
```

```python
import functools
import math

import jax
import jax.numpy as jnp
from jax import lax
from jax.experimental import pallas as pl
from jax.experimental.pallas import tpu as pltpu
from jax.sharding import PartitionSpec as P

CORE, Y, Z0 = 1, 2, 4
TEMPERATURE = 0.1
SCALE = 1.0 / TEMPERATURE
SCALE2 = SCALE * math.log2(math.e)
LANES = 128
F32, BF16 = jnp.float32, jnp.bfloat16
VMEM = pl.BlockSpec(memory_space=pltpu.VMEM)
ANY = pl.BlockSpec(memory_space=pl.ANY)


def grant(mib):
    return pltpu.CompilerParams(vmem_limit_bytes=mib * 2**20)


def cost(flops, nbytes, exps=0):
    return pl.CostEstimate(flops=flops, bytes_accessed=nbytes, transcendentals=exps)


def dot_nt(a, b):
    return lax.dot_general(a, b, (((1,), (1,)), ((), ())), preferred_element_type=F32)


def dot_tn(a, b):
    return lax.dot_general(a, b, (((0,), (0,)), ((), ())), preferred_element_type=F32)


def project_kernel(f_hbm, w_hbm, z_ref, ub_ref, f, w, sems):
    parts = sems.shape[0]
    depth = f.shape[1] // parts
    spans = [slice(k * depth, (k + 1) * depth) for k in range(parts)]
    copies = []
    for k, span in enumerate(spans):
        of_f = pltpu.make_async_copy(f_hbm.at[:, span], f.at[:, span], sems.at[k, 0])
        of_w = pltpu.make_async_copy(w_hbm.at[span], w.at[span], sems.at[k, 1])
        of_f.start()
        of_w.start()
        copies.append((of_f, of_w))
    z = jnp.zeros(z_ref.shape, F32)
    for span, (of_f, of_w) in zip(spans, copies):
        of_f.wait()
        of_w.wait()
        z = z + jnp.dot(f[:, span], w[span, :], preferred_element_type=F32)
    z_ref[...] = z
    inv = lax.rsqrt(jnp.sum(z * z, axis=1, keepdims=True) + 1e-06)
    ub_ref[...] = (z * inv).astype(BF16)


def project(feats, weight):
    rows, hid = feats.shape
    proj = weight.shape[1]
    return pl.pallas_call(
        project_kernel,
        in_specs=[ANY] * 2,
        out_specs=[VMEM] * 2,
        out_shape=[
            jax.ShapeDtypeStruct((rows, proj), F32),
            jax.ShapeDtypeStruct((rows, proj), BF16),
        ],
        scratch_shapes=[
            pltpu.VMEM((rows, hid), BF16),
            pltpu.VMEM((hid, proj), BF16),
            pltpu.SemaphoreType.DMA((8, 2)),
        ],
        cost_estimate=cost(2 * rows * hid * proj, 2 * hid * (rows + proj)),
        compiler_params=grant(53),
        name="project",
    )(feats, weight)


def fold_lanes(x):
    out = x[:, :LANES]
    for k in range(1, x.shape[1] // LANES):
        out = out + x[:, k * LANES : (k + 1) * LANES]
    return out


def fold_rows(x):
    return jnp.sum(x.reshape(x.shape[0] // 8, 8, x.shape[1]), axis=0)


def exp_scores(x, refs):
    y = jnp.concatenate([ref[...] for ref in refs], axis=0) if len(refs) > 1 else refs[0][...]
    return jnp.exp2(dot_nt(x, y) * SCALE2)


def den_kernel(n_old, n_new, first, *refs):
    total = n_old + n_new
    blocks = refs[:total]
    out_ref, col_acc, row_acc = refs[-3:]
    rows = blocks[0].shape[0]
    col_acc[...] = jnp.zeros_like(col_acc)
    even, odd = range(n_old, total, 2), range(n_old + 1, total, 2)
    for a in even:
        x = blocks[a][...]
        sums = jnp.zeros((rows, LANES), F32)
        for m in range(0, n_old, 2):
            e = exp_scores(x, blocks[m : m + 2])
            col_acc[:, m * rows : (m + 2) * rows] += fold_rows(e)
            sums = sums + fold_lanes(e)
        for m in odd:
            sums = sums + fold_lanes(exp_scores(x, [blocks[m]]))
        row_acc[(a - n_old) // 2] = sums
        for m in even:
            e = exp_scores(x, [blocks[m]])
            if m == a:
                line = lax.broadcasted_iota(jnp.int32, (rows, 1), 0)
                lane = lax.broadcasted_iota(jnp.int32, (1, rows), 1)
                e = jnp.where(line == lane, 0.0, e)
            col_acc[:, m * rows : (m + 1) * rows] += fold_rows(e)

    lane = lax.broadcasted_iota(jnp.int32, (rows, LANES), 1)
    turned = jnp.zeros((rows, LANES), F32)
    for k in range(len(even)):
        turned = jnp.where(lane == k, jnp.sum(row_acc[k], axis=1, keepdims=True), turned)
    turned = turned.T
    out_ref[...] = jnp.zeros_like(out_ref) if first else refs[total][...]
    for p in range(total):
        line = jnp.sum(col_acc[:, p * rows : (p + 1) * rows], axis=0, keepdims=True)
        if p in even:
            k = (p - n_old) // 2
            line = line + turned[k : k + 1, :]
        if p < n_old or p in even:
            out_ref[p : p + 1, :] += line


def partial_den(n_all, before, old, new):
    blocks = old + new
    rows, proj = blocks[0].shape
    total, n_new = len(blocks), len(new)
    turns = (n_new + 1) // 2
    pairs = turns * total
    return pl.pallas_call(
        functools.partial(den_kernel, len(old), n_new, before is None),
        in_specs=[VMEM] * (total + (before is not None)),
        out_specs=VMEM,
        out_shape=jax.ShapeDtypeStruct((n_all, rows), F32),
        scratch_shapes=[
            pltpu.VMEM((8, total * rows), F32),
            pltpu.VMEM((turns, rows, LANES), F32),
        ],
        cost_estimate=cost(0, 0),
        compiler_params=grant(8),
        name="partial_den",
    )(*blocks, *([] if before is None else [before]))


def as_column(line):
    return jnp.broadcast_to(line, (LANES, line.shape[1])).T[:, :1]


def as_line(column):
    return jnp.broadcast_to(column, (column.shape[0], LANES)).T[:1, :]


def partner_column(partner_ref):
    return as_column(partner_ref[...].astype(F32)).astype(jnp.int32)


def position():
    return lax.axis_index("blk"), lax.axis_index("group") & 1


def block_start(b, r, rows):
    return (b ^ r) * rows


def row_kernel(rs, first, partner_ref, x_ref, *refs):
    b, _ = position()
    n_all = len(rs)
    before, refs = (None, refs) if first == 0 else (refs[0], refs[1:])
    blocks, (e_ref, pos_ref), more = refs[:n_all], refs[n_all : n_all + 2], refs[n_all + 2 :]
    if more:
        cross = exp_scores(blocks[-2][...], blocks[-1:])
        more[0][0:1, :] = as_line(jnp.sum(fold_lanes(cross), axis=1, keepdims=True))
        more[0][1:2, :] = jnp.sum(cross, axis=0, keepdims=True)
    rows = x_ref.shape[0]
    partner = partner_column(partner_ref)
    x = x_ref[...]
    lane = lax.broadcasted_iota(jnp.int32, (1, rows), 1)
    line = lax.broadcasted_iota(jnp.int32, (rows, 1), 0)
    hits = jnp.zeros((rows, LANES), F32)
    for p in range(n_all):
        s = dot_nt(x, blocks[p][...])
        e = jnp.exp2(s * SCALE2)
        if first + p == 0:
            e = jnp.where(line == lane, 0.0, e)
        e_ref[:, p * rows : (p + 1) * rows] = e
        paired = (partner - block_start(b, rs[p], rows)) == lane
        hits = hits + fold_lanes(jnp.where(paired, s, 0.0))
    pos = as_line(jnp.sum(hits, axis=1, keepdims=True) * SCALE)
    pos_ref[...] = pos if before is None else pos + before[...]


def own_row(first, partner, x, before, blocks, rs):
    rows, proj = x.shape
    n = len(blocks)
    more = [] if first == 0 else [before]
    return pl.pallas_call(
        functools.partial(row_kernel, rs, first),
        in_specs=[VMEM] * (2 + len(more) + n),
        out_specs=[VMEM] * (2 + len(more)),
        out_shape=[
            jax.ShapeDtypeStruct((rows, n * rows), F32),
            jax.ShapeDtypeStruct((1, rows), F32),
        ]
        + [jax.ShapeDtypeStruct((2, rows), F32)] * len(more),
        cost_estimate=cost(0, 0),
        compiler_params=grant(8),
        name="own_row",
    )(partner, x, *more, *blocks)


def grad_kernel(rs, sizes, *refs):
    partner_ref, z_ref, mine_ref, theirs_ref, cross_ref = refs[:5]
    e_refs, refs = refs[5 : 5 + len(sizes)], refs[5 + len(sizes) :]
    b, _ = position()
    n_all = sum(sizes)
    e_at = [(ref, k) for ref, size in zip(e_refs, sizes) for k in range(size)]
    blocks, (lse_ref, dz_ref, dzb_ref, coef) = refs[:n_all], refs[n_all:]
    rows = z_ref.shape[0]
    den = [
        mine_ref[p : p + 1, :] + theirs_ref[p ^ 1 : (p ^ 1) + 1, :] for p in range(n_all)
    ]
    den[-2] = den[-2] + cross_ref[0:1, :]
    den[-1] = den[-1] + cross_ref[1:2, :]
    lse_ref[...] = jnp.log(den[0])
    inverse = [1.0 / line for line in den]
    own_inverse = as_column(inverse[0])
    partner = partner_column(partner_ref)
    lane = lax.broadcasted_iota(jnp.int32, (1, rows), 1)
    total = jnp.zeros(z_ref.shape, F32)
    part = 4
    for first in range(0, n_all, part):
        for p in range(first, first + part):
            span = slice(p * rows, (p + 1) * rows)
            paired = (partner - block_start(b, rs[p], rows)) == lane
            ref, k = e_at[p]
            e = ref[:, k * rows : (k + 1) * rows]
            h = e * (own_inverse + inverse[p]) - jnp.where(paired, 2.0, 0.0)
            coef[:, span] = h.astype(BF16)
        span = slice(first * rows, (first + part) * rows)
        x = jnp.concatenate([ref[...] for ref in blocks[first : first + part]], axis=0)
        total = total + jnp.dot(coef[:, span], x, preferred_element_type=F32)

    z = z_ref[...]
    inv = lax.rsqrt(jnp.sum(z * z, axis=1, keepdims=True) + 1e-06)
    u = z * inv
    g = total * SCALE
    dz = inv * (g - u * jnp.sum(u * g, axis=1, keepdims=True))
    dz_ref[...] = dz
    dzb_ref[...] = dz.astype(BF16)


def gradient(partner, z, mine, theirs, cross, es, blocks, rs):
    rows, proj = z.shape
    n = len(blocks)
    sizes = [e.shape[1] // rows for e in es]
    return pl.pallas_call(
        functools.partial(grad_kernel, rs, sizes),
        in_specs=[VMEM] * (5 + len(es) + n),
        out_specs=[VMEM] * 3,
        out_shape=[
            jax.ShapeDtypeStruct((1, rows), F32),
            jax.ShapeDtypeStruct((rows, proj), F32),
            jax.ShapeDtypeStruct((rows, proj), BF16),
        ],
        scratch_shapes=[pltpu.VMEM((rows, n * rows), BF16)],
        cost_estimate=cost(2 * n * rows * rows * proj, 6 * n * rows * proj),
        compiler_params=grant(12),
        name="gradient",
    )(partner, z, mine, theirs, cross, *es, *blocks)


def hand_out_kernel(*refs):
    n = len(refs) // 2
    for ref, out in zip(refs[:n], refs[n:]):
        out[...] = ref[...]


def hand_out(*arrays):
    return pl.pallas_call(
        hand_out_kernel,
        in_specs=[VMEM] * len(arrays),
        out_specs=[VMEM] * len(arrays),
        out_shape=[jax.ShapeDtypeStruct(x.shape, x.dtype) for x in arrays],
        cost_estimate=cost(0, 2 * sum(4 * x.size for x in arrays)),
        compiler_params=grant(4),
        name="hand_out",
    )(*arrays)


def head_kernel(planes, near, *refs):
    f_refs, d_refs = refs[:2], refs[2:4]
    keep, to_x, to_y, to_both = refs[4:]
    size = keep.shape[0]
    b, x = position()
    core, y, upper = b & 1, (b >> 1) & 1, (b // (Z0 * planes // 2)) & 1
    upper = upper if near else 1 - upper

    def product(x, y):
        at = (core * 8 + (x * 2 + y) * 2 + upper) * size
        span = pl.ds(pl.multiple_of(at, size), size)
        out = dot_tn(f_refs[0][:, span], d_refs[0][...])
        return out + dot_tn(f_refs[1][:, span], d_refs[1][...])

    to_both[...] = product(1 - x, 1 - y).astype(BF16)
    to_x[...] = product(1 - x, y).astype(BF16)
    to_y[...] = product(x, 1 - y).astype(BF16)
    keep[...] = product(x, y)


def head_partial(planes, near, fs, ds):
    rows, hid = fs[0].shape
    proj = ds[0].shape[1]
    shape = (hid // 16, proj)
    return pl.pallas_call(
        functools.partial(head_kernel, planes, near),
        in_specs=[VMEM] * 4,
        out_specs=[VMEM] * 4,
        out_shape=[jax.ShapeDtypeStruct(shape, t) for t in (F32, BF16, BF16, BF16)],
        cost_estimate=cost(hid * rows * proj, hid * proj),
        compiler_params=grant(8),
        name="head_partial",
    )(*fs, *ds)


def deal_kernel(near, keep, from_x, from_y, from_both, *refs):
    outs, total = refs[:-1], refs[-1]
    b, _ = position()
    n = len(outs)
    depth = total.shape[0] // n
    there = from_x[...].astype(F32) + from_y[...].astype(F32) + from_both[...].astype(F32)
    total[...] = keep[...] + there
    for k, out in enumerate(outs):
        place = ((b // Z0) ^ k) & (n - 1)
        chunk = total[pl.ds(pl.multiple_of(place * depth, depth), depth), :]
        out[...] = chunk.astype(out.dtype)


def deal(planes, near, keep, *got):
    rows, proj = keep.shape
    n = planes // 2
    kinds = [F32 if near and k == 0 else BF16 for k in range(n)]
    return pl.pallas_call(
        functools.partial(deal_kernel, near),
        in_specs=[VMEM] * 4,
        out_specs=[VMEM] * n,
        out_shape=[jax.ShapeDtypeStruct((rows // n, proj), t) for t in kinds],
        scratch_shapes=[pltpu.VMEM((rows, proj), F32)],
        cost_estimate=cost(0, 0),
        compiler_params=grant(4),
        name="deal",
    )(keep, *got)


def place_kernel(plan, planes, *refs):
    pieces, (out_ref, wide, sem) = refs[: len(plan)], refs[-3:]
    half = out_ref.shape[0] // 2
    b, side = position()
    copies = []
    for ref, (other, keys) in zip(pieces, plan):
        depth = ref.shape[1]
        core = (b & 1) ^ other
        for m, (s, r) in enumerate(keys):
            slot = len(copies)
            wide[slot] = ref[m].astype(F32)
            y = ((b >> 1) & 1) ^ ((r >> 1) & 1)
            plane = (b // Z0) ^ (r // Z0)
            at = core * half + (((side ^ s) * 2 + y) * planes + plane) * depth
            copy = pltpu.make_async_copy(
                wide.at[slot],
                out_ref.at[pl.ds(pl.multiple_of(at, depth), depth)],
                sem.at[slot],
            )
            copy.start()
            copies.append(copy)
    for copy in copies:
        copy.wait()


def place(planes, pieces, plan, shape, before=None):
    n = len(pieces)
    more = [] if before is None else [before]
    chunks = sum(len(keys) for _, keys in plan)
    return pl.pallas_call(
        functools.partial(place_kernel, plan, planes),
        in_specs=[VMEM] * n + [ANY] * len(more),
        out_specs=ANY,
        out_shape=jax.ShapeDtypeStruct(shape, F32),
        input_output_aliases={n: 0} if more else {},
        scratch_shapes=[
            pltpu.VMEM((chunks, *pieces[0].shape[1:]), F32),
            pltpu.SemaphoreType.DMA((chunks,)),
        ],
        cost_estimate=cost(0, 0),
        compiler_params=grant(8),
        name="place",
    )(*pieces, *more)


def gate(x, *after):
    return lax.optimization_barrier((x, *after))[0]


def swap(x, mask, axis, size):
    return lax.ppermute(x, axis, [(i, i ^ mask) for i in range(size)])


def on_device(n_blk, n_group, features, head_weight, pairs):
    feats = features[0]
    rows, hid = feats.shape
    proj = head_weight.shape[1]
    planes = n_blk // Z0

    def blk_swap(x, mask):
        return swap(x, mask, "blk", n_blk)

    def group_swap(x):
        return swap(x, 1, "group", n_group)

    def both_swap(x):
        moves = [
            (i * n_group + k, (i ^ Y) * n_group + (k ^ 1))
            for i in range(n_blk)
            for k in range(n_group)
        ]
        return lax.ppermute(x, ("blk", "group"), moves)

    z, ub = project(feats, head_weight)
    f_core = blk_swap(feats, CORE)

    seen, dens, es, pos = [], [], [], None

    def use(*new):
        before = dens[-1] if dens else None
        new = [item for pair in new for item in pair]
        dens.append(partial_den(n_blk, before, [x for x, _ in seen], [x for x, _ in new]))
        seen.extend(new)

    def take_row(start):
        blocks, rs = zip(*seen[start:])
        e, *rest = own_row(start, pairs, ub, pos, blocks, rs)
        es.append(e)
        return rest

    def pair(x, r, *after):
        return [(x, r), (blk_swap(gate(x, *after), CORE), r | CORE)]

    near, over_y = blk_swap(ub, Z0), blk_swap(ub, Y)
    if planes == 4:
        far = blk_swap(ub, 2 * Z0)
        mid = blk_swap(far, Z0)
        use(pair(ub, 0))
        near_y = blk_swap(gate(near, over_y), Y)
        use(pair(near, Z0))
        far_y = blk_swap(gate(far, dens[1]), Y)
        use(pair(over_y, Y), pair(far, 2 * Z0))
        mid_y = blk_swap(gate(mid, dens[2]), Y)
        use(pair(near_y, Z0 | Y), pair(far_y, 2 * Z0 | Y, mid), pair(mid, 3 * Z0))
        (pos,) = take_row(0)
        ending = pair(mid_y, 3 * Z0 | Y, dens[-1], es[-1])
    else:
        use(pair(ub, 0))
        waiting = pair(over_y, Y)
        for dz in range(1, planes):
            x = blk_swap(ub, dz * Z0)
            use(waiting, pair(x, dz * Z0))
            waiting = pair(blk_swap(x, Y), dz * Z0 | Y)
        (pos,) = take_row(0)
        ending = waiting

    use(ending[:1])
    seen.append(ending[1])
    theirs = blk_swap(dens[-1], CORE)
    pos, cross = take_row(es[0].shape[1] // rows)
    lse, grad_z, dz_own = gradient(
        pairs, z, dens[-1], theirs, cross, es, [x for x, _ in seen], [r for _, r in seen]
    )

    pos, lse, grad_z = hand_out(pos, lse, grad_z)
    fs, ds = [feats, f_core], [dz_own, blk_swap(dz_own, CORE)]
    n_half = planes // 2
    keep, *sends = head_partial(planes, False, fs, ds)
    sent = [group_swap(sends[0]), blk_swap(sends[1], Y), both_swap(sends[2])]
    far_sends = deal(planes, False, gate(keep, grad_z), *sent)
    got = [blk_swap(x, (n_half + k) * Z0) for k, x in enumerate(far_sends)]
    keep, *sends = head_partial(planes, True, fs, [gate(ds[0], keep), ds[1]])
    sent = [group_swap(sends[0]), blk_swap(sends[1], Y), both_swap(sends[2])]
    total, *near_sends = deal(planes, True, gate(keep, got[0]), *sent)
    got += [blk_swap(x, k * Z0) for k, x in enumerate(near_sends, 1)]
    for x in got:
        total = total + x.astype(F32)
    if n_group > 2:
        every = lax.all_gather(total, "group")
        side = lax.axis_index("group") & 1
        total = sum(jnp.where(side == i % 2, every[i], 0.0) for i in range(n_group))
    done = total.astype(BF16)

    line = [done] + [blk_swap(done, dz * Z0) for dz in range(1, planes)]

    def write(some, before):
        return place(
            planes, [x for x, _, _ in some], [some_of[1:] for some_of in some], (hid, proj), before
        )

    def swapped(some, *after):
        return [(blk_swap(gate(x, *after), CORE), 1, keys) for x, _, keys in some]

    head_total, sets = None, []
    for at in (0, n_half):
        part = jnp.stack(line[at : at + n_half])
        rs = [dz * Z0 for dz in range(at, at + n_half)]
        sets.append(
            [
                (part, 0, [(0, r) for r in rs]),
                (group_swap(part), 0, [(1, r) for r in rs]),
                (blk_swap(part, Y), 0, [(0, r | Y) for r in rs]),
                (both_swap(part), 0, [(1, r | Y) for r in rs]),
            ]
        )
    g = sets[0]
    head_total = write(g + swapped(g[:1]) + swapped(g[1:3], g[3][0]) + swapped(g[3:]), None)
    others = swapped(sets[1])
    head_total = write(sets[1] + others, head_total)
    return (pos, lse, grad_z[None, :, :], head_total)


def solution(mesh):
    n_blk, n_group = mesh.shape["blk"], mesh.shape["group"]

    def program(features, head_weight, pairs):
        return on_device(n_blk, n_group, features, head_weight, pairs)

    in_specs = (P("group", "blk", None), P(), P("group", "blk"))
    out_specs = (P("group", "blk"), P("group", "blk"), P("group", "blk", None), P())
    return jax.shard_map(
        program, mesh=mesh, in_specs=in_specs, out_specs=out_specs, check_vma=False
    )
```

```python
import functools
import math

import jax
import jax.numpy as jnp
from jax import lax
from jax.experimental import pallas as pl
from jax.experimental.pallas import tpu as pltpu
from jax.sharding import PartitionSpec as P

CORE, Y, Z0 = 1, 2, 4
TEMPERATURE = 0.1
SCALE = 1.0 / TEMPERATURE
SCALE2 = SCALE * math.log2(math.e)
LANES = 128
F32, BF16 = jnp.float32, jnp.bfloat16
VMEM = pl.BlockSpec(memory_space=pltpu.VMEM)
ANY = pl.BlockSpec(memory_space=pl.ANY)


def grant(mib):
    return pltpu.CompilerParams(vmem_limit_bytes=mib * 2**20)


def cost(flops, nbytes, exps=0):
    return pl.CostEstimate(flops=flops, bytes_accessed=nbytes, transcendentals=exps)


def dot_nt(a, b):
    return lax.dot_general(a, b, (((1,), (1,)), ((), ())), preferred_element_type=F32)


def dot_tn(a, b):
    return lax.dot_general(a, b, (((0,), (0,)), ((), ())), preferred_element_type=F32)


def project_kernel(f_hbm, w_hbm, z_ref, ub_ref, f, w, sems):
    parts = sems.shape[0]
    depth = f.shape[1] // parts
    spans = [slice(k * depth, (k + 1) * depth) for k in range(parts)]
    copies = []
    for k, span in enumerate(spans):
        of_f = pltpu.make_async_copy(f_hbm.at[:, span], f.at[:, span], sems.at[k, 0])
        of_w = pltpu.make_async_copy(w_hbm.at[span], w.at[span], sems.at[k, 1])
        of_f.start()
        of_w.start()
        copies.append((of_f, of_w))
    z = jnp.zeros(z_ref.shape, F32)
    for span, (of_f, of_w) in zip(spans, copies):
        of_f.wait()
        of_w.wait()
        z = z + jnp.dot(f[:, span], w[span, :], preferred_element_type=F32)
    z_ref[...] = z
    inv = lax.rsqrt(jnp.sum(z * z, axis=1, keepdims=True) + 1e-06)
    ub_ref[...] = (z * inv).astype(BF16)


def project(feats, weight):
    rows, hid = feats.shape
    proj = weight.shape[1]
    return pl.pallas_call(
        project_kernel,
        in_specs=[ANY] * 2,
        out_specs=[VMEM] * 2,
        out_shape=[
            jax.ShapeDtypeStruct((rows, proj), F32),
            jax.ShapeDtypeStruct((rows, proj), BF16),
        ],
        scratch_shapes=[
            pltpu.VMEM((rows, hid), BF16),
            pltpu.VMEM((hid, proj), BF16),
            pltpu.SemaphoreType.DMA((8, 2)),
        ],
        cost_estimate=cost(2 * rows * hid * proj, 2 * hid * (rows + proj)),
        compiler_params=grant(53),
        name="project",
    )(feats, weight)


def fold_lanes(x):
    out = x[:, :LANES]
    for k in range(1, x.shape[1] // LANES):
        out = out + x[:, k * LANES : (k + 1) * LANES]
    return out


def fold_rows(x):
    return jnp.sum(x.reshape(x.shape[0] // 8, 8, x.shape[1]), axis=0)


def exp_scores(x, refs):
    y = jnp.concatenate([ref[...] for ref in refs], axis=0) if len(refs) > 1 else refs[0][...]
    return jnp.exp2(dot_nt(x, y) * SCALE2)


def den_kernel(n_old, n_new, first, *refs):
    total = n_old + n_new
    blocks = refs[:total]
    out_ref, col_acc, row_acc = refs[-3:]
    rows = blocks[0].shape[0]
    col_acc[...] = jnp.zeros_like(col_acc)
    even, odd = range(n_old, total, 2), range(n_old + 1, total, 2)
    for a in even:
        x = blocks[a][...]
        sums = jnp.zeros((rows, LANES), F32)
        for m in range(0, n_old, 2):
            e = exp_scores(x, blocks[m : m + 2])
            col_acc[:, m * rows : (m + 2) * rows] += fold_rows(e)
            sums = sums + fold_lanes(e)
        for m in odd:
            sums = sums + fold_lanes(exp_scores(x, [blocks[m]]))
        row_acc[(a - n_old) // 2] = sums
        for m in even:
            e = exp_scores(x, [blocks[m]])
            if m == a:
                line = lax.broadcasted_iota(jnp.int32, (rows, 1), 0)
                lane = lax.broadcasted_iota(jnp.int32, (1, rows), 1)
                e = jnp.where(line == lane, 0.0, e)
            col_acc[:, m * rows : (m + 1) * rows] += fold_rows(e)

    lane = lax.broadcasted_iota(jnp.int32, (rows, LANES), 1)
    turned = jnp.zeros((rows, LANES), F32)
    for k in range(len(even)):
        turned = jnp.where(lane == k, jnp.sum(row_acc[k], axis=1, keepdims=True), turned)
    turned = turned.T
    out_ref[...] = jnp.zeros_like(out_ref) if first else refs[total][...]
    for p in range(total):
        line = jnp.sum(col_acc[:, p * rows : (p + 1) * rows], axis=0, keepdims=True)
        if p in even:
            k = (p - n_old) // 2
            line = line + turned[k : k + 1, :]
        if p < n_old or p in even:
            out_ref[p : p + 1, :] += line


def partial_den(n_all, before, old, new):
    blocks = old + new
    rows, proj = blocks[0].shape
    total, n_new = len(blocks), len(new)
    turns = (n_new + 1) // 2
    pairs = turns * total
    return pl.pallas_call(
        functools.partial(den_kernel, len(old), n_new, before is None),
        in_specs=[VMEM] * (total + (before is not None)),
        out_specs=VMEM,
        out_shape=jax.ShapeDtypeStruct((n_all, rows), F32),
        scratch_shapes=[
            pltpu.VMEM((8, total * rows), F32),
            pltpu.VMEM((turns, rows, LANES), F32),
        ],
        cost_estimate=cost(0, 0),
        compiler_params=grant(8),
        name="partial_den",
    )(*blocks, *([] if before is None else [before]))


def as_column(line):
    return jnp.broadcast_to(line, (LANES, line.shape[1])).T[:, :1]


def as_line(column):
    return jnp.broadcast_to(column, (column.shape[0], LANES)).T[:1, :]


def partner_column(partner_ref):
    return as_column(partner_ref[...].astype(F32)).astype(jnp.int32)


def position():
    return lax.axis_index("blk"), lax.axis_index("group") & 1


def block_start(b, r, rows):
    return (b ^ r) * rows


def row_kernel(rs, first, partner_ref, x_ref, *refs):
    b, _ = position()
    n_all = len(rs)
    before, refs = (None, refs) if first == 0 else (refs[0], refs[1:])
    blocks, (e_ref, pos_ref), more = refs[:n_all], refs[n_all : n_all + 2], refs[n_all + 2 :]
    if more:
        cross = exp_scores(blocks[-2][...], blocks[-1:])
        more[0][0:1, :] = as_line(jnp.sum(fold_lanes(cross), axis=1, keepdims=True))
        more[0][1:2, :] = jnp.sum(cross, axis=0, keepdims=True)
    rows = x_ref.shape[0]
    partner = partner_column(partner_ref)
    x = x_ref[...]
    lane = lax.broadcasted_iota(jnp.int32, (1, rows), 1)
    line = lax.broadcasted_iota(jnp.int32, (rows, 1), 0)
    hits = jnp.zeros((rows, LANES), F32)
    for p in range(n_all):
        s = dot_nt(x, blocks[p][...])
        e = jnp.exp2(s * SCALE2)
        if first + p == 0:
            e = jnp.where(line == lane, 0.0, e)
        e_ref[:, p * rows : (p + 1) * rows] = e
        paired = (partner - block_start(b, rs[p], rows)) == lane
        hits = hits + fold_lanes(jnp.where(paired, s, 0.0))
    pos = as_line(jnp.sum(hits, axis=1, keepdims=True) * SCALE)
    pos_ref[...] = pos if before is None else pos + before[...]


def own_row(first, partner, x, before, blocks, rs):
    rows, proj = x.shape
    n = len(blocks)
    more = [] if first == 0 else [before]
    return pl.pallas_call(
        functools.partial(row_kernel, rs, first),
        in_specs=[VMEM] * (2 + len(more) + n),
        out_specs=[VMEM] * (2 + len(more)),
        out_shape=[
            jax.ShapeDtypeStruct((rows, n * rows), F32),
            jax.ShapeDtypeStruct((1, rows), F32),
        ]
        + [jax.ShapeDtypeStruct((2, rows), F32)] * len(more),
        cost_estimate=cost(0, 0),
        compiler_params=grant(8),
        name="own_row",
    )(partner, x, *more, *blocks)


def grad_kernel(rs, sizes, *refs):
    partner_ref, z_ref, mine_ref, theirs_ref, cross_ref = refs[:5]
    e_refs, refs = refs[5 : 5 + len(sizes)], refs[5 + len(sizes) :]
    b, _ = position()
    n_all = sum(sizes)
    e_at = [(ref, k) for ref, size in zip(e_refs, sizes) for k in range(size)]
    blocks, (lse_ref, dz_ref, dzb_ref, coef) = refs[:n_all], refs[n_all:]
    rows = z_ref.shape[0]
    den = [
        mine_ref[p : p + 1, :] + theirs_ref[p ^ 1 : (p ^ 1) + 1, :] for p in range(n_all)
    ]
    den[-2] = den[-2] + cross_ref[0:1, :]
    den[-1] = den[-1] + cross_ref[1:2, :]
    lse_ref[...] = jnp.log(den[0])
    inverse = [1.0 / line for line in den]
    own_inverse = as_column(inverse[0])
    partner = partner_column(partner_ref)
    lane = lax.broadcasted_iota(jnp.int32, (1, rows), 1)
    total = jnp.zeros(z_ref.shape, F32)
    part = 4
    for first in range(0, n_all, part):
        for p in range(first, first + part):
            span = slice(p * rows, (p + 1) * rows)
            paired = (partner - block_start(b, rs[p], rows)) == lane
            ref, k = e_at[p]
            e = ref[:, k * rows : (k + 1) * rows]
            h = e * (own_inverse + inverse[p]) - jnp.where(paired, 2.0, 0.0)
            coef[:, span] = h.astype(BF16)
        span = slice(first * rows, (first + part) * rows)
        x = jnp.concatenate([ref[...] for ref in blocks[first : first + part]], axis=0)
        total = total + jnp.dot(coef[:, span], x, preferred_element_type=F32)

    z = z_ref[...]
    inv = lax.rsqrt(jnp.sum(z * z, axis=1, keepdims=True) + 1e-06)
    u = z * inv
    g = total * SCALE
    dz = inv * (g - u * jnp.sum(u * g, axis=1, keepdims=True))
    dz_ref[...] = dz
    dzb_ref[...] = dz.astype(BF16)


def gradient(partner, z, mine, theirs, cross, es, blocks, rs):
    rows, proj = z.shape
    n = len(blocks)
    sizes = [e.shape[1] // rows for e in es]
    return pl.pallas_call(
        functools.partial(grad_kernel, rs, sizes),
        in_specs=[VMEM] * (5 + len(es) + n),
        out_specs=[VMEM] * 3,
        out_shape=[
            jax.ShapeDtypeStruct((1, rows), F32),
            jax.ShapeDtypeStruct((rows, proj), F32),
            jax.ShapeDtypeStruct((rows, proj), BF16),
        ],
        scratch_shapes=[pltpu.VMEM((rows, n * rows), BF16)],
        cost_estimate=cost(2 * n * rows * rows * proj, 6 * n * rows * proj),
        compiler_params=grant(12),
        name="gradient",
    )(partner, z, mine, theirs, cross, *es, *blocks)


def hand_out_kernel(*refs):
    n = len(refs) // 2
    for ref, out in zip(refs[:n], refs[n:]):
        out[...] = ref[...]


def hand_out(*arrays):
    return pl.pallas_call(
        hand_out_kernel,
        in_specs=[VMEM] * len(arrays),
        out_specs=[VMEM] * len(arrays),
        out_shape=[jax.ShapeDtypeStruct(x.shape, x.dtype) for x in arrays],
        cost_estimate=cost(0, 2 * sum(4 * x.size for x in arrays)),
        compiler_params=grant(4),
        name="hand_out",
    )(*arrays)


def head_kernel(planes, near, *refs):
    f_refs, d_refs = refs[:2], refs[2:4]
    keep, to_x, to_y, to_both = refs[4:]
    size = keep.shape[0]
    b, x = position()
    core, y, upper = b & 1, (b >> 1) & 1, (b // (Z0 * planes // 2)) & 1
    upper = upper if near else 1 - upper

    def product(x, y):
        at = (core * 8 + (x * 2 + y) * 2 + upper) * size
        span = pl.ds(pl.multiple_of(at, size), size)
        out = dot_tn(f_refs[0][:, span], d_refs[0][...])
        return out + dot_tn(f_refs[1][:, span], d_refs[1][...])

    to_both[...] = product(1 - x, 1 - y).astype(BF16)
    to_x[...] = product(1 - x, y).astype(BF16)
    to_y[...] = product(x, 1 - y).astype(BF16)
    keep[...] = product(x, y)


def head_partial(planes, near, fs, ds):
    rows, hid = fs[0].shape
    proj = ds[0].shape[1]
    shape = (hid // 16, proj)
    return pl.pallas_call(
        functools.partial(head_kernel, planes, near),
        in_specs=[VMEM] * 4,
        out_specs=[VMEM] * 4,
        out_shape=[jax.ShapeDtypeStruct(shape, t) for t in (F32, BF16, BF16, BF16)],
        cost_estimate=cost(hid * rows * proj, hid * proj),
        compiler_params=grant(8),
        name="head_partial",
    )(*fs, *ds)


def deal_kernel(near, keep, from_x, from_y, from_both, *refs):
    outs, total = refs[:-1], refs[-1]
    b, _ = position()
    n = len(outs)
    depth = total.shape[0] // n
    there = from_x[...].astype(F32) + from_y[...].astype(F32) + from_both[...].astype(F32)
    total[...] = keep[...] + there
    for k, out in enumerate(outs):
        place = ((b // Z0) ^ k) & (n - 1)
        chunk = total[pl.ds(pl.multiple_of(place * depth, depth), depth), :]
        out[...] = chunk.astype(out.dtype)


def deal(planes, near, keep, *got):
    rows, proj = keep.shape
    n = planes // 2
    kinds = [F32 if near and k == 0 else BF16 for k in range(n)]
    return pl.pallas_call(
        functools.partial(deal_kernel, near),
        in_specs=[VMEM] * 4,
        out_specs=[VMEM] * n,
        out_shape=[jax.ShapeDtypeStruct((rows // n, proj), t) for t in kinds],
        scratch_shapes=[pltpu.VMEM((rows, proj), F32)],
        cost_estimate=cost(0, 0),
        compiler_params=grant(4),
        name="deal",
    )(keep, *got)


def place_kernel(plan, planes, *refs):
    pieces, (out_ref, wide, sem) = refs[: len(plan)], refs[-3:]
    half = out_ref.shape[0] // 2
    b, side = position()
    copies = []
    for ref, (other, keys) in zip(pieces, plan):
        depth = ref.shape[1]
        core = (b & 1) ^ other
        for m, (s, r) in enumerate(keys):
            slot = len(copies)
            wide[slot] = ref[m].astype(F32)
            y = ((b >> 1) & 1) ^ ((r >> 1) & 1)
            plane = (b // Z0) ^ (r // Z0)
            at = core * half + (((side ^ s) * 2 + y) * planes + plane) * depth
            copy = pltpu.make_async_copy(
                wide.at[slot],
                out_ref.at[pl.ds(pl.multiple_of(at, depth), depth)],
                sem.at[slot],
            )
            copy.start()
            copies.append(copy)
    for copy in copies:
        copy.wait()


def place(planes, pieces, plan, shape, before=None):
    n = len(pieces)
    more = [] if before is None else [before]
    chunks = sum(len(keys) for _, keys in plan)
    return pl.pallas_call(
        functools.partial(place_kernel, plan, planes),
        in_specs=[VMEM] * n + [ANY] * len(more),
        out_specs=ANY,
        out_shape=jax.ShapeDtypeStruct(shape, F32),
        input_output_aliases={n: 0} if more else {},
        scratch_shapes=[
            pltpu.VMEM((chunks, *pieces[0].shape[1:]), F32),
            pltpu.SemaphoreType.DMA((chunks,)),
        ],
        cost_estimate=cost(0, 0),
        compiler_params=grant(8),
        name="place",
    )(*pieces, *more)


def gate(x, *after):
    return lax.optimization_barrier((x, *after))[0]


def swap(x, mask, axis, size):
    return lax.ppermute(x, axis, [(i, i ^ mask) for i in range(size)])


def on_device(n_blk, n_group, features, head_weight, pairs):
    feats = features[0]
    rows, hid = feats.shape
    proj = head_weight.shape[1]
    planes = n_blk // Z0

    def blk_swap(x, mask):
        return swap(x, mask, "blk", n_blk)

    def group_swap(x):
        return swap(x, 1, "group", n_group)

    def both_swap(x):
        moves = [
            (i * n_group + k, (i ^ Y) * n_group + (k ^ 1))
            for i in range(n_blk)
            for k in range(n_group)
        ]
        return lax.ppermute(x, ("blk", "group"), moves)

    z, ub = project(feats, head_weight)
    f_core = blk_swap(feats, CORE)

    seen, dens, es, pos = [], [], [], None

    def use(*new):
        before = dens[-1] if dens else None
        new = [item for pair in new for item in pair]
        dens.append(partial_den(n_blk, before, [x for x, _ in seen], [x for x, _ in new]))
        seen.extend(new)

    def take_row(start):
        blocks, rs = zip(*seen[start:])
        e, *rest = own_row(start, pairs, ub, pos, blocks, rs)
        es.append(e)
        return rest

    def pair(x, r, *after):
        return [(x, r), (blk_swap(gate(x, *after), CORE), r | CORE)]

    near, over_y = blk_swap(ub, Z0), blk_swap(ub, Y)
    if planes == 4:
        far = blk_swap(ub, 2 * Z0)
        mid = blk_swap(far, Z0)
        use(pair(ub, 0))
        near_y = blk_swap(gate(near, over_y), Y)
        use(pair(near, Z0))
        far_y = blk_swap(gate(far, dens[1]), Y)
        use(pair(over_y, Y), pair(far, 2 * Z0))
        mid_y = blk_swap(mid, Y)
        use(pair(near_y, Z0 | Y), pair(far_y, 2 * Z0 | Y, mid), pair(mid, 3 * Z0, dens[2]))
        (pos,) = take_row(0)
        ending = pair(mid_y, 3 * Z0 | Y, dens[-1], es[-1])
    else:
        use(pair(ub, 0))
        waiting = pair(over_y, Y)
        for dz in range(1, planes):
            x = blk_swap(ub, dz * Z0)
            use(waiting, pair(x, dz * Z0))
            waiting = pair(blk_swap(x, Y), dz * Z0 | Y)
        (pos,) = take_row(0)
        ending = waiting

    use(ending[:1])
    seen.append(ending[1])
    theirs = blk_swap(dens[-1], CORE)
    pos, cross = take_row(es[0].shape[1] // rows)
    lse, grad_z, dz_own = gradient(
        pairs, z, dens[-1], theirs, cross, es, [x for x, _ in seen], [r for _, r in seen]
    )

    pos, lse, grad_z = hand_out(pos, lse, grad_z)
    fs, ds = [feats, f_core], [dz_own, blk_swap(dz_own, CORE)]
    n_half = planes // 2
    keep, *sends = head_partial(planes, False, fs, ds)
    sent = [group_swap(sends[0]), blk_swap(sends[1], Y), both_swap(sends[2])]
    far_sends = deal(planes, False, gate(keep, grad_z), *sent)
    got = [blk_swap(x, (n_half + k) * Z0) for k, x in enumerate(far_sends)]
    keep, *sends = head_partial(planes, True, fs, [gate(ds[0], keep), ds[1]])
    sent = [group_swap(sends[0]), blk_swap(sends[1], Y), both_swap(sends[2])]
    total, *near_sends = deal(planes, True, gate(keep, got[0]), *sent)
    got += [blk_swap(x, k * Z0) for k, x in enumerate(near_sends, 1)]
    for x in got:
        total = total + x.astype(F32)
    if n_group > 2:
        every = lax.all_gather(total, "group")
        side = lax.axis_index("group") & 1
        total = sum(jnp.where(side == i % 2, every[i], 0.0) for i in range(n_group))
    done = total.astype(BF16)

    line = [done] + [blk_swap(done, dz * Z0) for dz in range(1, planes)]

    def write(some, before):
        return place(
            planes, [x for x, _, _ in some], [some_of[1:] for some_of in some], (hid, proj), before
        )

    def swapped(some, *after):
        return [(blk_swap(gate(x, *after), CORE), 1, keys) for x, _, keys in some]

    sets = []
    for at in (0, n_half):
        part = jnp.stack(line[at : at + n_half])
        rs = [dz * Z0 for dz in range(at, at + n_half)]
        sets.append(
            [
                (group_swap(part), 0, [(1, r) for r in rs]),
                (blk_swap(part, Y), 0, [(0, r | Y) for r in rs]),
                (both_swap(part), 0, [(1, r | Y) for r in rs]),
            ]
        )
    own = [(jnp.stack(line), 0, [(0, dz * Z0) for dz in range(planes)])]
    b1, b2 = sets[0][2][0], sets[1][2][0]
    others = swapped(sets[0][:2], b1) + swapped(sets[0][2:]) + swapped(own, b1)
    head_total = write(own + sets[0] + others, None)
    others = swapped(sets[1][:2]) + swapped(sets[1][2:])
    head_total = write(sets[1] + others, head_total)
    return (pos, lse, grad_z[None, :, :], head_total)


def solution(mesh):
    n_blk, n_group = mesh.shape["blk"], mesh.shape["group"]

    def program(features, head_weight, pairs):
        return on_device(n_blk, n_group, features, head_weight, pairs)

    in_specs = (P("group", "blk", None), P(), P("group", "blk"))
    out_specs = (P("group", "blk"), P("group", "blk"), P("group", "blk", None), P())
    return jax.shard_map(
        program, mesh=mesh, in_specs=in_specs, out_specs=out_specs, check_vma=False
    )
```

```python
import functools
import math

import jax
import jax.numpy as jnp
from jax import lax
from jax.experimental import pallas as pl
from jax.experimental.pallas import tpu as pltpu
from jax.sharding import PartitionSpec as P

CORE, Y, Z0 = 1, 2, 4
TEMPERATURE = 0.1
SCALE = 1.0 / TEMPERATURE
SCALE2 = SCALE * math.log2(math.e)
LANES = 128
F32, BF16 = jnp.float32, jnp.bfloat16
VMEM = pl.BlockSpec(memory_space=pltpu.VMEM)
ANY = pl.BlockSpec(memory_space=pl.ANY)


def grant(mib):
    return pltpu.CompilerParams(vmem_limit_bytes=mib * 2**20)


def cost(flops, nbytes, exps=0):
    return pl.CostEstimate(flops=flops, bytes_accessed=nbytes, transcendentals=exps)


def dot_nt(a, b):
    return lax.dot_general(a, b, (((1,), (1,)), ((), ())), preferred_element_type=F32)


def dot_tn(a, b):
    return lax.dot_general(a, b, (((0,), (0,)), ((), ())), preferred_element_type=F32)


def project_kernel(f_hbm, w_hbm, z_ref, ub_ref, f, w, sems):
    parts = sems.shape[0]
    depth = f.shape[1] // parts
    spans = [slice(k * depth, (k + 1) * depth) for k in range(parts)]
    copies = []
    for k, span in enumerate(spans):
        of_f = pltpu.make_async_copy(f_hbm.at[:, span], f.at[:, span], sems.at[k, 0])
        of_w = pltpu.make_async_copy(w_hbm.at[span], w.at[span], sems.at[k, 1])
        of_f.start()
        of_w.start()
        copies.append((of_f, of_w))
    z = jnp.zeros(z_ref.shape, F32)
    for span, (of_f, of_w) in zip(spans, copies):
        of_f.wait()
        of_w.wait()
        z = z + jnp.dot(f[:, span], w[span, :], preferred_element_type=F32)
    z_ref[...] = z
    inv = lax.rsqrt(jnp.sum(z * z, axis=1, keepdims=True) + 1e-06)
    ub_ref[...] = (z * inv).astype(BF16)


def project(feats, weight):
    rows, hid = feats.shape
    proj = weight.shape[1]
    return pl.pallas_call(
        project_kernel,
        in_specs=[ANY] * 2,
        out_specs=[VMEM] * 2,
        out_shape=[
            jax.ShapeDtypeStruct((rows, proj), F32),
            jax.ShapeDtypeStruct((rows, proj), BF16),
        ],
        scratch_shapes=[
            pltpu.VMEM((rows, hid), BF16),
            pltpu.VMEM((hid, proj), BF16),
            pltpu.SemaphoreType.DMA((8, 2)),
        ],
        cost_estimate=cost(2 * rows * hid * proj, 2 * hid * (rows + proj)),
        compiler_params=grant(53),
        name="project",
    )(feats, weight)


def fold_lanes(x):
    out = x[:, :LANES]
    for k in range(1, x.shape[1] // LANES):
        out = out + x[:, k * LANES : (k + 1) * LANES]
    return out


def fold_rows(x):
    return jnp.sum(x.reshape(x.shape[0] // 8, 8, x.shape[1]), axis=0)


def exp_scores(x, refs):
    y = jnp.concatenate([ref[...] for ref in refs], axis=0) if len(refs) > 1 else refs[0][...]
    return jnp.exp2(dot_nt(x, y) * SCALE2)


def den_kernel(n_old, n_new, first, *refs):
    total = n_old + n_new
    blocks = refs[:total]
    out_ref, col_acc, row_acc = refs[-3:]
    rows = blocks[0].shape[0]
    col_acc[...] = jnp.zeros_like(col_acc)
    even, odd = range(n_old, total, 2), range(n_old + 1, total, 2)
    for a in even:
        x = blocks[a][...]
        sums = jnp.zeros((rows, LANES), F32)
        for m in range(0, n_old, 2):
            e = exp_scores(x, blocks[m : m + 2])
            col_acc[:, m * rows : (m + 2) * rows] += fold_rows(e)
            sums = sums + fold_lanes(e)
        for m in odd:
            sums = sums + fold_lanes(exp_scores(x, [blocks[m]]))
        row_acc[(a - n_old) // 2] = sums
        for m in even:
            e = exp_scores(x, [blocks[m]])
            if m == a:
                line = lax.broadcasted_iota(jnp.int32, (rows, 1), 0)
                lane = lax.broadcasted_iota(jnp.int32, (1, rows), 1)
                e = jnp.where(line == lane, 0.0, e)
            col_acc[:, m * rows : (m + 1) * rows] += fold_rows(e)

    lane = lax.broadcasted_iota(jnp.int32, (rows, LANES), 1)
    turned = jnp.zeros((rows, LANES), F32)
    for k in range(len(even)):
        turned = jnp.where(lane == k, jnp.sum(row_acc[k], axis=1, keepdims=True), turned)
    turned = turned.T
    out_ref[...] = jnp.zeros_like(out_ref) if first else refs[total][...]
    for p in range(total):
        line = jnp.sum(col_acc[:, p * rows : (p + 1) * rows], axis=0, keepdims=True)
        if p in even:
            k = (p - n_old) // 2
            line = line + turned[k : k + 1, :]
        if p < n_old or p in even:
            out_ref[p : p + 1, :] += line


def partial_den(n_all, before, old, new):
    blocks = old + new
    rows, proj = blocks[0].shape
    total, n_new = len(blocks), len(new)
    turns = (n_new + 1) // 2
    pairs = turns * total
    return pl.pallas_call(
        functools.partial(den_kernel, len(old), n_new, before is None),
        in_specs=[VMEM] * (total + (before is not None)),
        out_specs=VMEM,
        out_shape=jax.ShapeDtypeStruct((n_all, rows), F32),
        scratch_shapes=[
            pltpu.VMEM((8, total * rows), F32),
            pltpu.VMEM((turns, rows, LANES), F32),
        ],
        cost_estimate=cost(0, 0),
        compiler_params=grant(8),
        name="partial_den",
    )(*blocks, *([] if before is None else [before]))


def as_column(line):
    return jnp.broadcast_to(line, (LANES, line.shape[1])).T[:, :1]


def as_line(column):
    return jnp.broadcast_to(column, (column.shape[0], LANES)).T[:1, :]


def partner_column(partner_ref):
    return as_column(partner_ref[...].astype(F32)).astype(jnp.int32)


def position():
    return lax.axis_index("blk"), lax.axis_index("group") & 1


def block_start(b, r, rows):
    return (b ^ r) * rows


def row_kernel(rs, first, partner_ref, x_ref, *refs):
    b, _ = position()
    n_all = len(rs)
    before, refs = (None, refs) if first == 0 else (refs[0], refs[1:])
    blocks, (e_ref, pos_ref), more = refs[:n_all], refs[n_all : n_all + 2], refs[n_all + 2 :]
    if more:
        cross = exp_scores(blocks[-2][...], blocks[-1:])
        more[0][0:1, :] = as_line(jnp.sum(fold_lanes(cross), axis=1, keepdims=True))
        more[0][1:2, :] = jnp.sum(cross, axis=0, keepdims=True)
    rows = x_ref.shape[0]
    partner = partner_column(partner_ref)
    x = x_ref[...]
    lane = lax.broadcasted_iota(jnp.int32, (1, rows), 1)
    line = lax.broadcasted_iota(jnp.int32, (rows, 1), 0)
    hits = jnp.zeros((rows, LANES), F32)
    for p in range(n_all):
        s = dot_nt(x, blocks[p][...])
        e = jnp.exp2(s * SCALE2)
        if first + p == 0:
            e = jnp.where(line == lane, 0.0, e)
        e_ref[:, p * rows : (p + 1) * rows] = e
        paired = (partner - block_start(b, rs[p], rows)) == lane
        hits = hits + fold_lanes(jnp.where(paired, s, 0.0))
    pos = as_line(jnp.sum(hits, axis=1, keepdims=True) * SCALE)
    pos_ref[...] = pos if before is None else pos + before[...]


def own_row(first, partner, x, before, blocks, rs):
    rows, proj = x.shape
    n = len(blocks)
    more = [] if first == 0 else [before]
    return pl.pallas_call(
        functools.partial(row_kernel, rs, first),
        in_specs=[VMEM] * (2 + len(more) + n),
        out_specs=[VMEM] * (2 + len(more)),
        out_shape=[
            jax.ShapeDtypeStruct((rows, n * rows), F32),
            jax.ShapeDtypeStruct((1, rows), F32),
        ]
        + [jax.ShapeDtypeStruct((2, rows), F32)] * len(more),
        cost_estimate=cost(0, 0),
        compiler_params=grant(8),
        name="own_row",
    )(partner, x, *more, *blocks)


def grad_kernel(rs, sizes, *refs):
    partner_ref, z_ref, mine_ref, theirs_ref, cross_ref = refs[:5]
    e_refs, refs = refs[5 : 5 + len(sizes)], refs[5 + len(sizes) :]
    b, _ = position()
    n_all = sum(sizes)
    e_at = [(ref, k) for ref, size in zip(e_refs, sizes) for k in range(size)]
    blocks, (lse_ref, dz_ref, dzb_ref, coef) = refs[:n_all], refs[n_all:]
    rows = z_ref.shape[0]
    den = [
        mine_ref[p : p + 1, :] + theirs_ref[p ^ 1 : (p ^ 1) + 1, :] for p in range(n_all)
    ]
    den[-2] = den[-2] + cross_ref[0:1, :]
    den[-1] = den[-1] + cross_ref[1:2, :]
    lse_ref[...] = jnp.log(den[0])
    inverse = [1.0 / line for line in den]
    own_inverse = as_column(inverse[0])
    partner = partner_column(partner_ref)
    lane = lax.broadcasted_iota(jnp.int32, (1, rows), 1)
    total = jnp.zeros(z_ref.shape, F32)
    part = 4
    for first in range(0, n_all, part):
        for p in range(first, first + part):
            span = slice(p * rows, (p + 1) * rows)
            paired = (partner - block_start(b, rs[p], rows)) == lane
            ref, k = e_at[p]
            e = ref[:, k * rows : (k + 1) * rows]
            h = e * (own_inverse + inverse[p]) - jnp.where(paired, 2.0, 0.0)
            coef[:, span] = h.astype(BF16)
        span = slice(first * rows, (first + part) * rows)
        x = jnp.concatenate([ref[...] for ref in blocks[first : first + part]], axis=0)
        total = total + jnp.dot(coef[:, span], x, preferred_element_type=F32)

    z = z_ref[...]
    inv = lax.rsqrt(jnp.sum(z * z, axis=1, keepdims=True) + 1e-06)
    u = z * inv
    g = total * SCALE
    dz = inv * (g - u * jnp.sum(u * g, axis=1, keepdims=True))
    dz_ref[...] = dz
    dzb_ref[...] = dz.astype(BF16)


def gradient(partner, z, mine, theirs, cross, es, blocks, rs):
    rows, proj = z.shape
    n = len(blocks)
    sizes = [e.shape[1] // rows for e in es]
    return pl.pallas_call(
        functools.partial(grad_kernel, rs, sizes),
        in_specs=[VMEM] * (5 + len(es) + n),
        out_specs=[VMEM] * 3,
        out_shape=[
            jax.ShapeDtypeStruct((1, rows), F32),
            jax.ShapeDtypeStruct((rows, proj), F32),
            jax.ShapeDtypeStruct((rows, proj), BF16),
        ],
        scratch_shapes=[pltpu.VMEM((rows, n * rows), BF16)],
        cost_estimate=cost(2 * n * rows * rows * proj, 6 * n * rows * proj),
        compiler_params=grant(12),
        name="gradient",
    )(partner, z, mine, theirs, cross, *es, *blocks)


def hand_out_kernel(*refs):
    n = len(refs) // 2
    for ref, out in zip(refs[:n], refs[n:]):
        out[...] = ref[...]


def hand_out(*arrays):
    return pl.pallas_call(
        hand_out_kernel,
        in_specs=[VMEM] * len(arrays),
        out_specs=[VMEM] * len(arrays),
        out_shape=[jax.ShapeDtypeStruct(x.shape, x.dtype) for x in arrays],
        cost_estimate=cost(0, 2 * sum(4 * x.size for x in arrays)),
        compiler_params=grant(4),
        name="hand_out",
    )(*arrays)


def head_kernel(planes, near, *refs):
    f_refs, d_refs = refs[:2], refs[2:4]
    keep, to_x, to_y, to_both = refs[4:]
    size = keep.shape[0]
    b, x = position()
    core, y, upper = b & 1, (b >> 1) & 1, (b // (Z0 * planes // 2)) & 1
    upper = upper if near else 1 - upper

    def product(x, y):
        at = (core * 8 + (x * 2 + y) * 2 + upper) * size
        span = pl.ds(pl.multiple_of(at, size), size)
        out = dot_tn(f_refs[0][:, span], d_refs[0][...])
        return out + dot_tn(f_refs[1][:, span], d_refs[1][...])

    to_both[...] = product(1 - x, 1 - y).astype(BF16)
    to_x[...] = product(1 - x, y).astype(BF16)
    to_y[...] = product(x, 1 - y).astype(BF16)
    keep[...] = product(x, y)


def head_partial(planes, near, fs, ds):
    rows, hid = fs[0].shape
    proj = ds[0].shape[1]
    shape = (hid // 16, proj)
    return pl.pallas_call(
        functools.partial(head_kernel, planes, near),
        in_specs=[VMEM] * 4,
        out_specs=[VMEM] * 4,
        out_shape=[jax.ShapeDtypeStruct(shape, t) for t in (F32, BF16, BF16, BF16)],
        cost_estimate=cost(hid * rows * proj, hid * proj),
        compiler_params=grant(8),
        name="head_partial",
    )(*fs, *ds)


def deal_kernel(near, keep, from_x, from_y, from_both, *refs):
    outs, total = refs[:-1], refs[-1]
    b, _ = position()
    n = len(outs)
    depth = total.shape[0] // n
    there = from_x[...].astype(F32) + from_y[...].astype(F32) + from_both[...].astype(F32)
    total[...] = keep[...] + there
    for k, out in enumerate(outs):
        place = ((b // Z0) ^ k) & (n - 1)
        chunk = total[pl.ds(pl.multiple_of(place * depth, depth), depth), :]
        out[...] = chunk.astype(out.dtype)


def deal(planes, near, keep, *got):
    rows, proj = keep.shape
    n = planes // 2
    kinds = [F32 if near and k == 0 else BF16 for k in range(n)]
    return pl.pallas_call(
        functools.partial(deal_kernel, near),
        in_specs=[VMEM] * 4,
        out_specs=[VMEM] * n,
        out_shape=[jax.ShapeDtypeStruct((rows // n, proj), t) for t in kinds],
        scratch_shapes=[pltpu.VMEM((rows, proj), F32)],
        cost_estimate=cost(0, 0),
        compiler_params=grant(4),
        name="deal",
    )(keep, *got)


def place_kernel(plan, planes, *refs):
    pieces, (out_ref, wide, sem) = refs[: len(plan)], refs[-3:]
    half = out_ref.shape[0] // 2
    b, side = position()
    copies = []
    for ref, (other, keys) in zip(pieces, plan):
        depth = ref.shape[1]
        core = (b & 1) ^ other
        for m, (s, r) in enumerate(keys):
            slot = len(copies)
            wide[slot] = ref[m].astype(F32)
            y = ((b >> 1) & 1) ^ ((r >> 1) & 1)
            plane = (b // Z0) ^ (r // Z0)
            at = core * half + (((side ^ s) * 2 + y) * planes + plane) * depth
            copy = pltpu.make_async_copy(
                wide.at[slot],
                out_ref.at[pl.ds(pl.multiple_of(at, depth), depth)],
                sem.at[slot],
            )
            copy.start()
            copies.append(copy)
    for copy in copies:
        copy.wait()


def place(planes, pieces, plan, shape, before=None):
    n = len(pieces)
    more = [] if before is None else [before]
    chunks = sum(len(keys) for _, keys in plan)
    return pl.pallas_call(
        functools.partial(place_kernel, plan, planes),
        in_specs=[VMEM] * n + [ANY] * len(more),
        out_specs=ANY,
        out_shape=jax.ShapeDtypeStruct(shape, F32),
        input_output_aliases={n: 0} if more else {},
        scratch_shapes=[
            pltpu.VMEM((chunks, *pieces[0].shape[1:]), F32),
            pltpu.SemaphoreType.DMA((chunks,)),
        ],
        cost_estimate=cost(0, 0),
        compiler_params=grant(8),
        name="place",
    )(*pieces, *more)


def gate(x, *after):
    return lax.optimization_barrier((x, *after))[0]


def swap(x, mask, axis, size):
    return lax.ppermute(x, axis, [(i, i ^ mask) for i in range(size)])


def on_device(n_blk, n_group, features, head_weight, pairs):
    feats = features[0]
    rows, hid = feats.shape
    proj = head_weight.shape[1]
    planes = n_blk // Z0

    def blk_swap(x, mask):
        return swap(x, mask, "blk", n_blk)

    def group_swap(x):
        return swap(x, 1, "group", n_group)

    def both_swap(x):
        moves = [
            (i * n_group + k, (i ^ Y) * n_group + (k ^ 1))
            for i in range(n_blk)
            for k in range(n_group)
        ]
        return lax.ppermute(x, ("blk", "group"), moves)

    z, ub = project(feats, head_weight)
    f_core = blk_swap(feats, CORE)

    seen, dens, es, pos = [], [], [], None

    def use(*new):
        before = dens[-1] if dens else None
        new = [item for pair in new for item in pair]
        dens.append(partial_den(n_blk, before, [x for x, _ in seen], [x for x, _ in new]))
        seen.extend(new)

    def take_row(start):
        blocks, rs = zip(*seen[start:])
        e, *rest = own_row(start, pairs, ub, pos, blocks, rs)
        es.append(e)
        return rest

    def pair(x, r, *after):
        return [(x, r), (blk_swap(gate(x, *after), CORE), r | CORE)]

    near, over_y = blk_swap(ub, Z0), blk_swap(ub, Y)
    if planes == 4:
        far = blk_swap(ub, 2 * Z0)
        mid = blk_swap(far, Z0)
        use(pair(ub, 0))
        near_y = blk_swap(gate(near, over_y), Y)
        use(pair(near, Z0))
        far_y = blk_swap(gate(far, dens[1]), Y)
        use(pair(over_y, Y), pair(far, 2 * Z0))
        mid_y = blk_swap(mid, Y)
        use(pair(near_y, Z0 | Y), pair(far_y, 2 * Z0 | Y, mid), pair(mid, 3 * Z0))
        (pos,) = take_row(0)
        ending = pair(mid_y, 3 * Z0 | Y, dens[-1], es[-1])
    else:
        use(pair(ub, 0))
        waiting = pair(over_y, Y)
        for dz in range(1, planes):
            x = blk_swap(ub, dz * Z0)
            use(waiting, pair(x, dz * Z0))
            waiting = pair(blk_swap(x, Y), dz * Z0 | Y)
        (pos,) = take_row(0)
        ending = waiting

    use(ending[:1])
    seen.append(ending[1])
    theirs = blk_swap(dens[-1], CORE)
    pos, cross = take_row(es[0].shape[1] // rows)
    lse, grad_z, dz_own = gradient(
        pairs, z, dens[-1], theirs, cross, es, [x for x, _ in seen], [r for _, r in seen]
    )

    pos, lse, grad_z = hand_out(pos, lse, grad_z)
    fs, ds = [feats, f_core], [dz_own, blk_swap(dz_own, CORE)]
    n_half = planes // 2
    keep, *sends = head_partial(planes, False, fs, ds)
    sent = [group_swap(sends[0]), blk_swap(sends[1], Y), both_swap(sends[2])]
    far_sends = deal(planes, False, gate(keep, grad_z), *sent)
    got = [blk_swap(x, (n_half + k) * Z0) for k, x in enumerate(far_sends)]
    keep, *sends = head_partial(planes, True, fs, [gate(ds[0], keep), ds[1]])
    sent = [group_swap(sends[0]), blk_swap(sends[1], Y), both_swap(sends[2])]
    total, *near_sends = deal(planes, True, gate(keep, got[0]), *sent)
    got += [blk_swap(x, k * Z0) for k, x in enumerate(near_sends, 1)]
    for x in got:
        total = total + x.astype(F32)
    if n_group > 2:
        every = lax.all_gather(total, "group")
        side = lax.axis_index("group") & 1
        total = sum(jnp.where(side == i % 2, every[i], 0.0) for i in range(n_group))
    done = total.astype(BF16)

    line = [done] + [blk_swap(done, dz * Z0) for dz in range(1, planes)]

    def write(some, before):
        return place(
            planes, [x for x, _, _ in some], [some_of[1:] for some_of in some], (hid, proj), before
        )

    def swapped(some, *after):
        return [(blk_swap(gate(x, *after), CORE), 1, keys) for x, _, keys in some]

    sets = []
    for at in (0, n_half):
        part = jnp.stack(line[at : at + n_half])
        rs = [dz * Z0 for dz in range(at, at + n_half)]
        sets.append(
            [
                (group_swap(part), 0, [(1, r) for r in rs]),
                (blk_swap(part, Y), 0, [(0, r | Y) for r in rs]),
                (both_swap(part), 0, [(1, r | Y) for r in rs]),
            ]
        )
    own = [(jnp.stack(line), 0, [(0, dz * Z0) for dz in range(planes)])]
    b1, b2 = sets[0][2][0], sets[1][2][0]
    others = swapped(sets[0][:2], b1) + swapped(sets[0][2:]) + swapped(own, b1)
    head_total = write(own + sets[0] + others, None)
    others = swapped(sets[1][:2]) + swapped(sets[1][2:])
    head_total = write(sets[1] + others, head_total)
    return (pos, lse, grad_z[None, :, :], head_total)


def solution(mesh):
    n_blk, n_group = mesh.shape["blk"], mesh.shape["group"]

    def program(features, head_weight, pairs):
        return on_device(n_blk, n_group, features, head_weight, pairs)

    in_specs = (P("group", "blk", None), P(), P("group", "blk"))
    out_specs = (P("group", "blk"), P("group", "blk"), P("group", "blk", None), P())
    return jax.shard_map(
        program, mesh=mesh, in_specs=in_specs, out_specs=out_specs, check_vma=False
    )
```

```python
import functools
import math

import jax
import jax.numpy as jnp
from jax import lax
from jax.experimental import pallas as pl
from jax.experimental.pallas import tpu as pltpu
from jax.sharding import PartitionSpec as P

CORE, Y, Z0 = 1, 2, 4
TEMPERATURE = 0.1
SCALE = 1.0 / TEMPERATURE
SCALE2 = SCALE * math.log2(math.e)
LANES = 128
F32, BF16 = jnp.float32, jnp.bfloat16
VMEM = pl.BlockSpec(memory_space=pltpu.VMEM)
ANY = pl.BlockSpec(memory_space=pl.ANY)


def grant(mib):
    return pltpu.CompilerParams(vmem_limit_bytes=mib * 2**20)


def cost(flops, nbytes, exps=0):
    return pl.CostEstimate(flops=flops, bytes_accessed=nbytes, transcendentals=exps)


def dot_nt(a, b):
    return lax.dot_general(a, b, (((1,), (1,)), ((), ())), preferred_element_type=F32)


def dot_tn(a, b):
    return lax.dot_general(a, b, (((0,), (0,)), ((), ())), preferred_element_type=F32)


def project_kernel(f_hbm, w_hbm, z_ref, ub_ref, f, w, sems):
    parts = sems.shape[0]
    depth = f.shape[1] // parts
    spans = [slice(k * depth, (k + 1) * depth) for k in range(parts)]
    copies = []
    for k, span in enumerate(spans):
        of_f = pltpu.make_async_copy(f_hbm.at[:, span], f.at[:, span], sems.at[k, 0])
        of_w = pltpu.make_async_copy(w_hbm.at[span], w.at[span], sems.at[k, 1])
        of_f.start()
        of_w.start()
        copies.append((of_f, of_w))
    z = jnp.zeros(z_ref.shape, F32)
    for span, (of_f, of_w) in zip(spans, copies):
        of_f.wait()
        of_w.wait()
        z = z + jnp.dot(f[:, span], w[span, :], preferred_element_type=F32)
    z_ref[...] = z
    inv = lax.rsqrt(jnp.sum(z * z, axis=1, keepdims=True) + 1e-06)
    ub_ref[...] = (z * inv).astype(BF16)


def project(feats, weight):
    rows, hid = feats.shape
    proj = weight.shape[1]
    return pl.pallas_call(
        project_kernel,
        in_specs=[ANY] * 2,
        out_specs=[VMEM] * 2,
        out_shape=[
            jax.ShapeDtypeStruct((rows, proj), F32),
            jax.ShapeDtypeStruct((rows, proj), BF16),
        ],
        scratch_shapes=[
            pltpu.VMEM((rows, hid), BF16),
            pltpu.VMEM((hid, proj), BF16),
            pltpu.SemaphoreType.DMA((8, 2)),
        ],
        cost_estimate=cost(2 * rows * hid * proj, 2 * hid * (rows + proj)),
        compiler_params=grant(53),
        name="project",
    )(feats, weight)


def fold_lanes(x):
    out = x[:, :LANES]
    for k in range(1, x.shape[1] // LANES):
        out = out + x[:, k * LANES : (k + 1) * LANES]
    return out


def fold_rows(x):
    return jnp.sum(x.reshape(x.shape[0] // 8, 8, x.shape[1]), axis=0)


def exp_scores(x, refs):
    y = jnp.concatenate([ref[...] for ref in refs], axis=0) if len(refs) > 1 else refs[0][...]
    return jnp.exp2(dot_nt(x, y) * SCALE2)


def den_kernel(n_old, n_new, first, *refs):
    total = n_old + n_new
    blocks = refs[:total]
    out_ref, col_acc, row_acc = refs[-3:]
    rows = blocks[0].shape[0]
    col_acc[...] = jnp.zeros_like(col_acc)
    even, odd = range(n_old, total, 2), range(n_old + 1, total, 2)
    for a in even:
        x = blocks[a][...]
        sums = jnp.zeros((rows, LANES), F32)
        for m in range(0, n_old, 2):
            e = exp_scores(x, blocks[m : m + 2])
            col_acc[:, m * rows : (m + 2) * rows] += fold_rows(e)
            sums = sums + fold_lanes(e)
        for m in odd:
            sums = sums + fold_lanes(exp_scores(x, [blocks[m]]))
        row_acc[(a - n_old) // 2] = sums
        for m in even:
            e = exp_scores(x, [blocks[m]])
            if m == a:
                line = lax.broadcasted_iota(jnp.int32, (rows, 1), 0)
                lane = lax.broadcasted_iota(jnp.int32, (1, rows), 1)
                e = jnp.where(line == lane, 0.0, e)
            col_acc[:, m * rows : (m + 1) * rows] += fold_rows(e)

    lane = lax.broadcasted_iota(jnp.int32, (rows, LANES), 1)
    turned = jnp.zeros((rows, LANES), F32)
    for k in range(len(even)):
        turned = jnp.where(lane == k, jnp.sum(row_acc[k], axis=1, keepdims=True), turned)
    turned = turned.T
    out_ref[...] = jnp.zeros_like(out_ref) if first else refs[total][...]
    for p in range(total):
        line = jnp.sum(col_acc[:, p * rows : (p + 1) * rows], axis=0, keepdims=True)
        if p in even:
            k = (p - n_old) // 2
            line = line + turned[k : k + 1, :]
        if p < n_old or p in even:
            out_ref[p : p + 1, :] += line


def partial_den(n_all, before, old, new):
    blocks = old + new
    rows, proj = blocks[0].shape
    total, n_new = len(blocks), len(new)
    turns = (n_new + 1) // 2
    pairs = turns * total
    return pl.pallas_call(
        functools.partial(den_kernel, len(old), n_new, before is None),
        in_specs=[VMEM] * (total + (before is not None)),
        out_specs=VMEM,
        out_shape=jax.ShapeDtypeStruct((n_all, rows), F32),
        scratch_shapes=[
            pltpu.VMEM((8, total * rows), F32),
            pltpu.VMEM((turns, rows, LANES), F32),
        ],
        cost_estimate=cost(0, 0),
        compiler_params=grant(8),
        name="partial_den",
    )(*blocks, *([] if before is None else [before]))


def as_column(line):
    return jnp.broadcast_to(line, (LANES, line.shape[1])).T[:, :1]


def as_line(column):
    return jnp.broadcast_to(column, (column.shape[0], LANES)).T[:1, :]


def partner_column(partner_ref):
    return as_column(partner_ref[...].astype(F32)).astype(jnp.int32)


def position():
    return lax.axis_index("blk"), lax.axis_index("group") & 1


def block_start(b, r, rows):
    return (b ^ r) * rows


def row_kernel(rs, first, partner_ref, x_ref, *refs):
    b, _ = position()
    n_all = len(rs)
    before, refs = (None, refs) if first == 0 else (refs[0], refs[1:])
    blocks, (e_ref, pos_ref), more = refs[:n_all], refs[n_all : n_all + 2], refs[n_all + 2 :]
    if more:
        cross = exp_scores(blocks[-2][...], blocks[-1:])
        more[0][0:1, :] = as_line(jnp.sum(fold_lanes(cross), axis=1, keepdims=True))
        more[0][1:2, :] = jnp.sum(cross, axis=0, keepdims=True)
    rows = x_ref.shape[0]
    partner = partner_column(partner_ref)
    x = x_ref[...]
    lane = lax.broadcasted_iota(jnp.int32, (1, rows), 1)
    line = lax.broadcasted_iota(jnp.int32, (rows, 1), 0)
    hits = jnp.zeros((rows, LANES), F32)
    for p in range(n_all):
        s = dot_nt(x, blocks[p][...])
        e = jnp.exp2(s * SCALE2)
        if first + p == 0:
            e = jnp.where(line == lane, 0.0, e)
        e_ref[:, p * rows : (p + 1) * rows] = e
        paired = (partner - block_start(b, rs[p], rows)) == lane
        hits = hits + fold_lanes(jnp.where(paired, s, 0.0))
    pos = as_line(jnp.sum(hits, axis=1, keepdims=True) * SCALE)
    pos_ref[...] = pos if before is None else pos + before[...]


def own_row(first, partner, x, before, blocks, rs):
    rows, proj = x.shape
    n = len(blocks)
    more = [] if first == 0 else [before]
    return pl.pallas_call(
        functools.partial(row_kernel, rs, first),
        in_specs=[VMEM] * (2 + len(more) + n),
        out_specs=[VMEM] * (2 + len(more)),
        out_shape=[
            jax.ShapeDtypeStruct((rows, n * rows), F32),
            jax.ShapeDtypeStruct((1, rows), F32),
        ]
        + [jax.ShapeDtypeStruct((2, rows), F32)] * len(more),
        cost_estimate=cost(0, 0),
        compiler_params=grant(8),
        name="own_row",
    )(partner, x, *more, *blocks)


def grad_kernel(rs, sizes, *refs):
    partner_ref, z_ref, mine_ref, theirs_ref, cross_ref = refs[:5]
    e_refs, refs = refs[5 : 5 + len(sizes)], refs[5 + len(sizes) :]
    b, _ = position()
    n_all = sum(sizes)
    e_at = [(ref, k) for ref, size in zip(e_refs, sizes) for k in range(size)]
    blocks, (lse_ref, dz_ref, dzb_ref, coef) = refs[:n_all], refs[n_all:]
    rows = z_ref.shape[0]
    den = [
        mine_ref[p : p + 1, :] + theirs_ref[p ^ 1 : (p ^ 1) + 1, :] for p in range(n_all)
    ]
    den[-2] = den[-2] + cross_ref[0:1, :]
    den[-1] = den[-1] + cross_ref[1:2, :]
    lse_ref[...] = jnp.log(den[0])
    inverse = [1.0 / line for line in den]
    own_inverse = as_column(inverse[0])
    partner = partner_column(partner_ref)
    lane = lax.broadcasted_iota(jnp.int32, (1, rows), 1)
    total = jnp.zeros(z_ref.shape, F32)
    part = 4
    for first in range(0, n_all, part):
        for p in range(first, first + part):
            span = slice(p * rows, (p + 1) * rows)
            paired = (partner - block_start(b, rs[p], rows)) == lane
            ref, k = e_at[p]
            e = ref[:, k * rows : (k + 1) * rows]
            h = e * (own_inverse + inverse[p]) - jnp.where(paired, 2.0, 0.0)
            coef[:, span] = h.astype(BF16)
        span = slice(first * rows, (first + part) * rows)
        x = jnp.concatenate([ref[...] for ref in blocks[first : first + part]], axis=0)
        total = total + jnp.dot(coef[:, span], x, preferred_element_type=F32)

    z = z_ref[...]
    inv = lax.rsqrt(jnp.sum(z * z, axis=1, keepdims=True) + 1e-06)
    u = z * inv
    g = total * SCALE
    dz = inv * (g - u * jnp.sum(u * g, axis=1, keepdims=True))
    dz_ref[...] = dz
    dzb_ref[...] = dz.astype(BF16)


def gradient(partner, z, mine, theirs, cross, es, blocks, rs):
    rows, proj = z.shape
    n = len(blocks)
    sizes = [e.shape[1] // rows for e in es]
    return pl.pallas_call(
        functools.partial(grad_kernel, rs, sizes),
        in_specs=[VMEM] * (5 + len(es) + n),
        out_specs=[VMEM] * 3,
        out_shape=[
            jax.ShapeDtypeStruct((1, rows), F32),
            jax.ShapeDtypeStruct((rows, proj), F32),
            jax.ShapeDtypeStruct((rows, proj), BF16),
        ],
        scratch_shapes=[pltpu.VMEM((rows, n * rows), BF16)],
        cost_estimate=cost(2 * n * rows * rows * proj, 6 * n * rows * proj),
        compiler_params=grant(12),
        name="gradient",
    )(partner, z, mine, theirs, cross, *es, *blocks)


def hand_out_kernel(*refs):
    n = len(refs) // 2
    for ref, out in zip(refs[:n], refs[n:]):
        out[...] = ref[...]


def hand_out(*arrays):
    return pl.pallas_call(
        hand_out_kernel,
        in_specs=[VMEM] * len(arrays),
        out_specs=[VMEM] * len(arrays),
        out_shape=[jax.ShapeDtypeStruct(x.shape, x.dtype) for x in arrays],
        cost_estimate=cost(0, 2 * sum(4 * x.size for x in arrays)),
        compiler_params=grant(4),
        name="hand_out",
    )(*arrays)


def head_kernel(planes, near, *refs):
    f_refs, d_refs = refs[:2], refs[2:4]
    keep, to_x, to_y, to_both = refs[4:]
    size = keep.shape[0]
    b, x = position()
    core, y, upper = b & 1, (b >> 1) & 1, (b // (Z0 * planes // 2)) & 1
    upper = upper if near else 1 - upper

    def product(x, y):
        at = (core * 8 + (x * 2 + y) * 2 + upper) * size
        span = pl.ds(pl.multiple_of(at, size), size)
        out = dot_tn(f_refs[0][:, span], d_refs[0][...])
        return out + dot_tn(f_refs[1][:, span], d_refs[1][...])

    to_both[...] = product(1 - x, 1 - y).astype(BF16)
    to_x[...] = product(1 - x, y).astype(BF16)
    to_y[...] = product(x, 1 - y).astype(BF16)
    keep[...] = product(x, y)


def head_partial(planes, near, fs, ds):
    rows, hid = fs[0].shape
    proj = ds[0].shape[1]
    shape = (hid // 16, proj)
    return pl.pallas_call(
        functools.partial(head_kernel, planes, near),
        in_specs=[VMEM] * 4,
        out_specs=[VMEM] * 4,
        out_shape=[jax.ShapeDtypeStruct(shape, t) for t in (F32, BF16, BF16, BF16)],
        cost_estimate=cost(hid * rows * proj, hid * proj),
        compiler_params=grant(8),
        name="head_partial",
    )(*fs, *ds)


def deal_kernel(near, keep, from_x, from_y, from_both, *refs):
    outs, total = refs[:-1], refs[-1]
    b, _ = position()
    n = len(outs)
    depth = total.shape[0] // n
    there = from_x[...].astype(F32) + from_y[...].astype(F32) + from_both[...].astype(F32)
    total[...] = keep[...] + there
    for k, out in enumerate(outs):
        place = ((b // Z0) ^ k) & (n - 1)
        chunk = total[pl.ds(pl.multiple_of(place * depth, depth), depth), :]
        out[...] = chunk.astype(out.dtype)


def deal(planes, near, keep, *got):
    rows, proj = keep.shape
    n = planes // 2
    kinds = [F32 if near and k == 0 else BF16 for k in range(n)]
    return pl.pallas_call(
        functools.partial(deal_kernel, near),
        in_specs=[VMEM] * 4,
        out_specs=[VMEM] * n,
        out_shape=[jax.ShapeDtypeStruct((rows // n, proj), t) for t in kinds],
        scratch_shapes=[pltpu.VMEM((rows, proj), F32)],
        cost_estimate=cost(0, 0),
        compiler_params=grant(4),
        name="deal",
    )(keep, *got)


def place_kernel(plan, planes, *refs):
    pieces, (out_ref, wide, sem) = refs[: len(plan)], refs[-3:]
    half = out_ref.shape[0] // 2
    b, side = position()
    copies = []
    for ref, (other, keys) in zip(pieces, plan):
        depth = ref.shape[1]
        core = (b & 1) ^ other
        for m, (s, r) in enumerate(keys):
            slot = len(copies)
            wide[slot] = ref[m].astype(F32)
            y = ((b >> 1) & 1) ^ ((r >> 1) & 1)
            plane = (b // Z0) ^ (r // Z0)
            at = core * half + (((side ^ s) * 2 + y) * planes + plane) * depth
            copy = pltpu.make_async_copy(
                wide.at[slot],
                out_ref.at[pl.ds(pl.multiple_of(at, depth), depth)],
                sem.at[slot],
            )
            copy.start()
            copies.append(copy)
    for copy in copies:
        copy.wait()


def place(planes, pieces, plan, shape, before=None):
    n = len(pieces)
    more = [] if before is None else [before]
    chunks = sum(len(keys) for _, keys in plan)
    return pl.pallas_call(
        functools.partial(place_kernel, plan, planes),
        in_specs=[VMEM] * n + [ANY] * len(more),
        out_specs=ANY,
        out_shape=jax.ShapeDtypeStruct(shape, F32),
        input_output_aliases={n: 0} if more else {},
        scratch_shapes=[
            pltpu.VMEM((chunks, *pieces[0].shape[1:]), F32),
            pltpu.SemaphoreType.DMA((chunks,)),
        ],
        cost_estimate=cost(0, 0),
        compiler_params=grant(8),
        name="place",
    )(*pieces, *more)


def gate(x, *after):
    return lax.optimization_barrier((x, *after))[0]


def swap(x, mask, axis, size):
    return lax.ppermute(x, axis, [(i, i ^ mask) for i in range(size)])


def on_device(n_blk, n_group, features, head_weight, pairs):
    feats = features[0]
    rows, hid = feats.shape
    proj = head_weight.shape[1]
    planes = n_blk // Z0

    def blk_swap(x, mask):
        return swap(x, mask, "blk", n_blk)

    def group_swap(x):
        return swap(x, 1, "group", n_group)

    def both_swap(x):
        moves = [
            (i * n_group + k, (i ^ Y) * n_group + (k ^ 1))
            for i in range(n_blk)
            for k in range(n_group)
        ]
        return lax.ppermute(x, ("blk", "group"), moves)

    z, ub = project(feats, head_weight)
    f_core = blk_swap(feats, CORE)

    seen, dens, es, pos = [], [], [], None

    def use(*new):
        before = dens[-1] if dens else None
        new = [item for pair in new for item in pair]
        dens.append(partial_den(n_blk, before, [x for x, _ in seen], [x for x, _ in new]))
        seen.extend(new)

    def take_row(start):
        blocks, rs = zip(*seen[start:])
        e, *rest = own_row(start, pairs, ub, pos, blocks, rs)
        es.append(e)
        return rest

    def pair(x, r, *after):
        return [(x, r), (blk_swap(gate(x, *after), CORE), r | CORE)]

    near, over_y = blk_swap(ub, Z0), blk_swap(ub, Y)
    if planes == 4:
        far = blk_swap(ub, 2 * Z0)
        mid = blk_swap(far, Z0)
        use(pair(ub, 0))
        near_y = blk_swap(gate(near, over_y), Y)
        use(pair(near, Z0))
        far_y = blk_swap(gate(far, dens[1]), Y)
        use(pair(over_y, Y), pair(far, 2 * Z0, near_y))
        mid_y = blk_swap(mid, Y)
        use(pair(near_y, Z0 | Y), pair(far_y, 2 * Z0 | Y, mid), pair(mid, 3 * Z0))
        (pos,) = take_row(0)
        ending = pair(mid_y, 3 * Z0 | Y, dens[-1], es[-1])
    else:
        use(pair(ub, 0))
        waiting = pair(over_y, Y)
        for dz in range(1, planes):
            x = blk_swap(ub, dz * Z0)
            use(waiting, pair(x, dz * Z0))
            waiting = pair(blk_swap(x, Y), dz * Z0 | Y)
        (pos,) = take_row(0)
        ending = waiting

    use(ending[:1])
    seen.append(ending[1])
    theirs = blk_swap(dens[-1], CORE)
    pos, cross = take_row(es[0].shape[1] // rows)
    lse, grad_z, dz_own = gradient(
        pairs, z, dens[-1], theirs, cross, es, [x for x, _ in seen], [r for _, r in seen]
    )

    pos, lse, grad_z = hand_out(pos, lse, grad_z)
    fs, ds = [feats, f_core], [dz_own, blk_swap(dz_own, CORE)]
    n_half = planes // 2
    keep, *sends = head_partial(planes, False, fs, ds)
    sent = [group_swap(sends[0]), blk_swap(sends[1], Y), both_swap(sends[2])]
    far_sends = deal(planes, False, gate(keep, grad_z), *sent)
    got = [blk_swap(x, (n_half + k) * Z0) for k, x in enumerate(far_sends)]
    keep, *sends = head_partial(planes, True, fs, [gate(ds[0], keep), ds[1]])
    sent = [group_swap(sends[0]), blk_swap(sends[1], Y), both_swap(sends[2])]
    total, *near_sends = deal(planes, True, gate(keep, got[0]), *sent)
    got += [blk_swap(x, k * Z0) for k, x in enumerate(near_sends, 1)]
    for x in got:
        total = total + x.astype(F32)
    if n_group > 2:
        every = lax.all_gather(total, "group")
        side = lax.axis_index("group") & 1
        total = sum(jnp.where(side == i % 2, every[i], 0.0) for i in range(n_group))
    done = total.astype(BF16)

    line = [done] + [blk_swap(done, dz * Z0) for dz in range(1, planes)]

    def write(some, before):
        return place(
            planes, [x for x, _, _ in some], [some_of[1:] for some_of in some], (hid, proj), before
        )

    def swapped(some, *after):
        return [(blk_swap(gate(x, *after), CORE), 1, keys) for x, _, keys in some]

    sets = []
    for at in (0, n_half):
        part = jnp.stack(line[at : at + n_half])
        rs = [dz * Z0 for dz in range(at, at + n_half)]
        sets.append(
            [
                (group_swap(part), 0, [(1, r) for r in rs]),
                (blk_swap(part, Y), 0, [(0, r | Y) for r in rs]),
                (both_swap(part), 0, [(1, r | Y) for r in rs]),
            ]
        )
    own = [(jnp.stack(line), 0, [(0, dz * Z0) for dz in range(planes)])]
    b1, b2 = sets[0][2][0], sets[1][2][0]
    others = swapped(sets[0][:2], b1) + swapped(sets[0][2:]) + swapped(own, b1)
    head_total = write(own + sets[0] + others, None)
    others = swapped(sets[1][:2]) + swapped(sets[1][2:])
    head_total = write(sets[1] + others, head_total)
    return (pos, lse, grad_z[None, :, :], head_total)


def solution(mesh):
    n_blk, n_group = mesh.shape["blk"], mesh.shape["group"]

    def program(features, head_weight, pairs):
        return on_device(n_blk, n_group, features, head_weight, pairs)

    in_specs = (P("group", "blk", None), P(), P("group", "blk"))
    out_specs = (P("group", "blk"), P("group", "blk"), P("group", "blk", None), P())
    return jax.shard_map(
        program, mesh=mesh, in_specs=in_specs, out_specs=out_specs, check_vma=False
    )
```
